256 devices in a mesh: pa: 16 (over x, z_lo, core), pb: 16 (over y, z_hi).
Axes of the slice: x: 4, y: 4, z: 8 (z_hi: 4, z_lo: 2; z = z_hi * 2 + z_lo), core: 2. Of those that a mesh axis runs over, the one named last changes fastest.
Arguments:
- point_keys: bfloat16 [32768, 768], P(('pa', 'pb')), may hold values from -7 to 7
- point_values: bfloat16 [32768, 768], P(('pa', 'pb')), may hold values from -40 to 40
- out_grad: bfloat16 [32768, 768], P(('pa', 'pb')), may hold values from -512 to 512
- decoder_norm: float32 [12, 32768], P(None, ('pa', 'pb')), as said below
- latent_query: bfloat16 [1024, 768], P(('pa', 'pb')), may hold values from -4 to 4
- latent_out: bfloat16 [1024, 768], P(('pa', 'pb')), may hold values from -5 to 5
- encoder_norm: float32 [12, 1024], replicated, as said below
Outputs:
- keys_grad: bfloat16 [32768, 768], P(('pa', 'pb'))
- values_grad: bfloat16 [32768, 768], P(('pa', 'pb'))
- latent_grad: float32 [1024, 768], P(('pa', 'pb'))
The draws below stay inside these ranges and needn't reach their ends.
Inputs may be any that keep to these rules, and one draw needn't show every extreme that they name: `decoder_norm`: each entry lies between log(1024) - 0.3 and log(1024) + 1.3. `encoder_norm`: each entry lies between log(32768) - 0.3 and log(32768) + 1.3.
All inputs are finite; a program needn't handle non-finite values.
Results may differ from the reference program's by a relative error of at most 0.004.
The reference program's roundings to bfloat16 on the way count: a program that leaves them out, or rounds other values in their place, can miss the bound.
Values may be sent and summed in bfloat16 or wider, within the bound.
A program may use at most 64 MiB of HBM per device.

```python
import math
import jax
import jax.numpy as jnp
from jax import lax

HEADS = 12
HEAD_DIM = 64
LATENTS = 1024
TOK_DEV = 128
D = 768
POINTS = 32768


def shared_queries(key):
    raw = jnp.clip(jax.random.normal(jax.random.fold_in(key, 51), (LATENTS, D), jnp.float32), -3.5, 3.5)
    raw = raw.reshape(LATENTS, HEADS, HEAD_DIM)
    length = jnp.sqrt(jnp.sum(raw * raw, axis=2, keepdims=True)) + 1e-06
    unit = raw * (math.sqrt(HEAD_DIM) / length)
    return jnp.clip(unit.reshape(LATENTS, D), -4.0, 4.0)


def draw_latent_query(key, part):
    return shared_queries(key).astype(jnp.bfloat16)


def draw_point_keys(key, part):
    groups = POINTS // TOK_DEV
    per_owner = LATENTS // groups
    queries = shared_queries(key)
    positions = jnp.arange(POINTS, dtype=jnp.int32)
    device = positions // TOK_DEV
    local = positions % TOK_DEV
    offsets = jax.random.randint(jax.random.fold_in(key, 52), (groups,), 1, groups, dtype=jnp.int32)
    far_owner = (device + groups // 2) % groups
    other_owner = (device + offsets[device]) % groups
    owner = jnp.where(local % 2 == 0, far_owner, other_owner)
    pick = jax.random.randint(jax.random.fold_in(key, 53), (POINTS,), 0, per_owner, dtype=jnp.int32)
    target = (owner * per_owner + pick).astype(jnp.int32)
    aligned = queries[target]
    noise = jnp.clip(jax.random.normal(jax.random.fold_in(key, 54), (POINTS, D), jnp.float32), -4.0, 4.0)
    mixed = 0.6 * noise + 0.8 * aligned
    return jnp.clip(mixed, -7.0, 7.0).astype(jnp.bfloat16)


def draw_point_values(key, part):
    base = jnp.clip(jax.random.normal(jax.random.fold_in(key, 11), (POINTS, D), jnp.float32), -4.0, 4.0)
    rising = 1.0 + 2.0 * jnp.arange(POINTS, dtype=jnp.float32)[:, None] / POINTS
    row_scale = jnp.exp(jax.random.uniform(jax.random.fold_in(key, 12), (POINTS, 1), jnp.float32, 0.0, math.log(10.0))) / 3.0
    return jnp.clip(base * rising * row_scale, -40.0, 40.0).astype(jnp.bfloat16)


def draw_out_grad(key, part):
    scale_factor = LATENTS // 8
    base = jnp.clip(jax.random.normal(jax.random.fold_in(key, 23), (POINTS, D), jnp.float32), -4.0, 4.0)
    return (base * scale_factor).astype(jnp.bfloat16)


def draw_decoder_norm(key, part):
    spread = jax.random.uniform(jax.random.fold_in(key, 32), (HEADS, POINTS), jnp.float32, 0.0, 1.0)
    return (math.log(LATENTS) + spread).astype(jnp.float32)


def draw_encoder_norm(key, part):
    spread = jax.random.uniform(jax.random.fold_in(key, 42), (HEADS, LATENTS), jnp.float32, 0.0, 1.0)
    return (math.log(POINTS) + spread).astype(jnp.float32)


def levels(key, extent, shards, smallest, top_value):
    factor_of = 1.0
    for position, parts in shards:
        steps = jax.random.uniform(jax.random.fold_in(jax.random.fold_in(key, 6), position), (parts,), jnp.float32, smallest / len(shards), top_value / len(shards))
        factor_of = factor_of * jnp.repeat(jnp.exp(steps), extent[position] // parts).reshape((-1,) + (1,) * (len(extent) - 1 - position))
    return factor_of


def centred(own_key, dims, width, bound, split=(), kind=jnp.bfloat16):
    array = width * jax.random.normal(own_key, dims, jnp.float32)
    if split:
        array = array * levels(own_key, dims, split, -0.22, 0.18)
    return jnp.clip(array, -bound, bound).astype(kind)


def setup_inputs(seed: int = 0) -> dict:
    keys = jax.random.split(jax.random.key(seed), 8)
    point_keys = draw_point_keys(jax.random.fold_in(keys[7], 71), 0)
    point_values = draw_point_values(jax.random.fold_in(keys[7], 71), 0)
    out_grad = draw_out_grad(jax.random.fold_in(keys[7], 71), 0)
    decoder_norm = draw_decoder_norm(jax.random.fold_in(keys[7], 71), 0)
    latent_query = draw_latent_query(jax.random.fold_in(keys[7], 71), 0)
    latent_out = centred(keys[5], (LATENTS, D), 1.0, 5.0, ((0, 256),))
    encoder_norm = draw_encoder_norm(jax.random.fold_in(keys[7], 71), 0)
    return {"point_keys": point_keys, "point_values": point_values, "out_grad": out_grad, "decoder_norm": decoder_norm, "latent_query": latent_query, "latent_out": latent_out, "encoder_norm": encoder_norm}


PRECISION_MAXIMUM = lax.Precision.HIGHEST


def divide_heads(block):
    return block.astype(jnp.float32).reshape(block.shape[0], HEADS, HEAD_DIM)


def rounded_portion(block):
    return lax.optimization_barrier(block.astype(jnp.bfloat16)).astype(jnp.float32)


def reference(point_keys, point_values, out_grad, decoder_norm, latent_query, latent_out, encoder_norm):
    scale_factor = HEAD_DIM ** -0.5
    latent_head_rows = divide_heads(latent_query)
    output_heads = divide_heads(latent_out)
    blocks = POINTS // TOK_DEV
    key_blocks = point_keys.reshape(blocks, TOK_DEV, D)
    value_blocks = point_values.reshape(blocks, TOK_DEV, D)
    grad_blocks = out_grad.reshape(blocks, TOK_DEV, D)
    norm_blocks = decoder_norm.reshape(HEADS, blocks, TOK_DEV).transpose(1, 0, 2)

    def scores_of(key_tile_block):
        return jnp.einsum("cxt,ext->xce", divide_heads(key_tile_block), latent_head_rows, precision=PRECISION_MAXIMUM) * scale_factor

    def pass_one(state, inputs):
        key_tile_block, grad_block, norm_block = inputs
        key_head_rows = divide_heads(key_tile_block)
        gradient_heads = divide_heads(grad_block)
        decoder_weights = jnp.exp(scores_of(key_tile_block) - norm_block[:, :, None])
        decoder_gradient = jnp.einsum("cxt,ext->xce", gradient_heads, output_heads, precision=PRECISION_MAXIMUM)
        row_total = jnp.sum(decoder_weights * decoder_gradient, axis=2, keepdims=True)
        decoder_scores_grad = rounded_portion(decoder_weights * (decoder_gradient - row_total))
        mixing_piece = jnp.einsum("lzb,zly->bly", rounded_portion(decoder_weights), gradient_heads, precision=PRECISION_MAXIMUM)
        query_portion = jnp.einsum("lzb,zly->bly", decoder_scores_grad, key_head_rows, precision=PRECISION_MAXIMUM) * scale_factor
        key_portion = jnp.einsum("qjx,xqi->jqi", decoder_scores_grad, latent_head_rows, precision=PRECISION_MAXIMUM) * scale_factor
        return (state[0] + mixing_piece, state[1] + query_portion), key_portion

    blank = jnp.zeros((LATENTS, HEADS, HEAD_DIM), jnp.float32)
    (mix_grad, query_grad), key_decoder = lax.scan(pass_one, (blank, blank), (key_blocks, grad_blocks, norm_blocks))
    mixing_portion = rounded_portion(mix_grad)

    def encoder_of(key_tile_block, value_tile_block):
        encoder = jnp.exp(scores_of(key_tile_block) - encoder_norm[:, None, :])
        encoder_gradient = jnp.einsum("cxt,ext->xce", divide_heads(value_tile_block), mixing_portion, precision=PRECISION_MAXIMUM)
        return encoder, encoder_gradient

    def pass_two(state, inputs):
        key_tile_block, value_tile_block = inputs
        encoder, encoder_gradient = encoder_of(key_tile_block, value_tile_block)
        encoder_portion = rounded_portion(encoder)
        value_portion = jnp.einsum("qjx,xqi->jqi", encoder_portion, mixing_portion, precision=PRECISION_MAXIMUM)
        return state + jnp.sum(encoder_portion * encoder_gradient, axis=1), value_portion.astype(jnp.bfloat16)

    column_total, value_grad = lax.scan(pass_two, jnp.zeros((HEADS, LATENTS), jnp.float32), (key_blocks, value_blocks))

    def pass_three(state, inputs):
        key_tile_block, value_tile_block, key_before = inputs
        encoder, encoder_gradient = encoder_of(key_tile_block, value_tile_block)
        encoder_scores_grad = rounded_portion(encoder * (encoder_gradient - column_total[:, None, :]))
        query_portion = jnp.einsum("lzb,zly->bly", encoder_scores_grad, divide_heads(key_tile_block), precision=PRECISION_MAXIMUM) * scale_factor
        key_portion = jnp.einsum("qjx,xqi->jqi", encoder_scores_grad, latent_head_rows, precision=PRECISION_MAXIMUM) * scale_factor
        return state + query_portion, (key_before + key_portion).astype(jnp.bfloat16)

    query_grad, key_grad = lax.scan(pass_three, query_grad, (key_blocks, value_blocks, key_decoder))
    return key_grad.reshape(POINTS, D), value_grad.reshape(POINTS, D), query_grad.reshape(LATENTS, D)
```

```python
import jax
import jax.numpy as jnp
from jax import lax
from jax.experimental import pallas as pl
from jax.experimental.pallas import tpu as pltpu
from jax.sharding import PartitionSpec as P

HEADS = 12
HEAD_DIM = 64
SLOTS = 16
PTS = 128
BLOCK = 64
CHUNK = 4
CROWS = CHUNK * BLOCK
NB = 4
NW = 512
MESH = pl.DeviceIdType.MESH
F32 = jnp.float32
BF16 = jnp.bfloat16


def dot(a, b):
    return jnp.dot(a, b, preferred_element_type=F32)


def three_terms(v):
    one = v.astype(BF16).astype(F32)
    two = (v - one).astype(BF16).astype(F32)
    three = (v - one - two).astype(BF16).astype(F32)
    return one, two, three


def iota(shape, dim):
    return lax.broadcasted_iota(jnp.int32, shape, dim)


def kernel(
    keys_ref, values_ref, grad_ref, dnorm_ref, query_ref, lout_ref, enorm_ref,
    kout_ref, vout_ref, lgout_ref,
    send_lat, send_pts, tall, got_lat, got_pts,
    key_rows, grad_rows, value_rows, key_grad, value_cols, dnorm, enorm,
    lat, lat_turned, dec, enc, dgrad, query_acc,
    mixu, from_core, summed, from_z, mix_all, keys_t, values_t,
    lg_part, lg_core, lg_summed, lg_z, lg_own, kv_send, kv_got, lg_got,
    s_lat, r_lat, s_pts, r_pts, s_all, r_all, s_core, r_core, s_z, r_z,
    s_mix, r_mix, s_core2, r_core2, s_z2, r_z2, s_kv, r_kv, s_lg, r_lg,
):
    pa, pb = lax.axis_index("pa"), lax.axis_index("pb")
    x, zlo, c = pa // 4, (pa // 2) % 2, pa % 2
    y, zhi = pb // 4, pb % 4
    z = zhi * 2 + zlo
    slot = x * 4 + y
    member = c * 8 + z

    def in_plane(t):
        return ((t // 4) * 4 + zlo * 2 + c, (t % 4) * 4 + zhi)

    def in_column(g):
        cc, zz = g // 8, g % 8
        return (x * 4 + (zz % 2) * 2 + cc, y * 4 + zz // 2)

    def remote(src, dst, s, r, to):
        return pltpu.make_async_remote_copy(
            src_ref=src, dst_ref=dst, send_sem=s, recv_sem=r, device_id=to, device_id_type=MESH
        )

    def loop(lo, hi, body):
        def step(i, carry):
            body(i)
            return carry

        lax.fori_loop(lo, hi, step, 0)

    barrier = pltpu.get_barrier_semaphore()

    def greet(k):
        pl.semaphore_signal(barrier, inc=1, device_id=in_plane((slot + k) % SLOTS), device_id_type=MESH)
        pl.semaphore_signal(barrier, inc=1, device_id=in_column((member + k) % SLOTS), device_id_type=MESH)

    loop(1, SLOTS, greet)

    for k in range(4):
        tall[0, 4 * k : 4 * k + 4, :] = query_ref[...].astype(F32) * 0.125
        tall[1, 4 * k : 4 * k + 4, :] = lout_ref[...].astype(F32)
    rows16 = iota((16, 128), 0)
    left16 = iota((16, 128), 1) < HEAD_DIM
    mine = rows16 // 4 == y
    for p in range(HEADS // 2):
        q = tall[0, :, 128 * p : 128 * p + 128]
        o = tall[1, :, 128 * p : 128 * p + 128]
        even = jnp.where(left16, q, pltpu.roll(o, HEAD_DIM, 1))
        odd = jnp.where(left16, pltpu.roll(q, HEAD_DIM, 1), o)
        send_lat[2 * p, 0:16, :] = jnp.where(mine, even, 0.0).astype(BF16)
        send_lat[2 * p + 1, 0:16, :] = jnp.where(mine, odd, 0.0).astype(BF16)
    for h in range(HEADS):
        one, two, three = three_terms(dnorm_ref[h : h + 1, :])
        send_lat[h, 16:32, :] = jnp.where(
            rows16 == 0, one, jnp.where(rows16 == 1, two, jnp.where(rows16 == 2, three, 0.0))
        ).astype(BF16)

    for p in range(HEADS // 2):
        for i, ref in enumerate((keys_ref, grad_ref, values_ref)):
            turned = jnp.transpose(ref[:, 128 * p : 128 * p + 128])
            send_pts[2 * p, 64 * i : 64 * i + 64, :] = turned[0:64]
            send_pts[2 * p + 1, 64 * i : 64 * i + 64, :] = turned[64:128]

    pl.semaphore_wait(barrier, 2 * (SLOTS - 1))

    def lat_copy(h, src_slot):
        return remote(send_lat.at[h], got_lat.at[src_slot], s_lat.at[h], r_lat.at[src_slot], in_plane(h))

    def pts_copy(h, src_slot):
        return remote(send_pts.at[h], got_pts.at[src_slot], s_pts.at[h], r_pts.at[src_slot], in_plane(h))

    def to_heads(copy):
        def body(k):
            h = (slot + k) % SLOTS

            @pl.when(h < HEADS)
            def _():
                copy(h, slot).start()

        loop(1, SLOTS, body)

    to_heads(lat_copy)
    to_heads(pts_copy)

    @pl.when(slot < HEADS)
    def _():
        got_lat[slot] = send_lat[slot]
        got_pts[slot] = send_pts[slot]

        norm_row = enorm_ref[pl.ds(slot, 1), :]
        terms = three_terms(norm_row)

        def norm_block(g):
            cc, zz = g // 8, g % 8
            r = iota((BLOCK, 1024), 0)
            place = (r // 16) * 256 + (zz % 2) * 128 + cc * 64 + ((r // 4) % 4) * 16 + (zz // 2) * 4 + r % 4
            hot = jnp.where(iota((BLOCK, 1024), 1) == place, 1.0, 0.0).astype(BF16)
            total = jnp.zeros((BLOCK, 128), F32)
            for t in terms:
                wide = jnp.broadcast_to(t, (128, 1024)).astype(BF16)
                total = total + lax.dot_general(
                    hot, wide, (((1,), (1,)), ((), ())), preferred_element_type=F32
                )
            enorm[g] = total

        loop(0, SLOTS, norm_block)

        zero_rows = jnp.zeros((HEAD_DIM, NW), BF16)
        ones_rows = jnp.where(iota((HEAD_DIM, NW), 0) < 3, -1.0, 0.0).astype(BF16)
        for b in range(NB):
            key_rows[b, 64:128, :] = zero_rows
            grad_rows[b, 0:64, :] = zero_rows
            value_rows[b, 64:128, :] = ones_rows

        def lat_wait(k):
            lat_copy(slot, (slot + k) % SLOTS).wait_recv()

        loop(1, SLOTS, lat_wait)

        for i in range(4):
            total = got_lat[4 * i, 0:16, :].astype(F32)
            for j in range(1, 4):
                total = total + got_lat[4 * i + j, 0:16, :].astype(F32)
            lat[member, 16 * i : 16 * i + 16, :] = total.astype(BF16)

        def all_copy(buf, s, r, g_to, g_from):
            return remote(buf.at[g_from], buf.at[g_from], s.at[g_to], r.at[g_from], in_column(g_to))

        loop(1, SLOTS, lambda k: all_copy(lat, s_all, r_all, (member + k) % SLOTS, member).start())

        for t in range(SLOTS):
            dn = jnp.sum(got_lat[t, 16:32, :].astype(F32), axis=0, keepdims=True)
            dnorm[t // 4, :, 128 * (t % 4) : 128 * (t % 4) + 128] = jnp.broadcast_to(dn, (8, 128))

        def pts_wait(k):
            pts_copy(slot, (slot + k) % SLOTS).wait_recv()

        loop(1, SLOTS, pts_wait)

        for t in range(SLOTS):
            b, at = t // 4, 128 * (t % 4)
            key_rows[b, 0:64, at : at + 128] = got_pts[t, 0:64, :]
            grad_rows[b, 64:128, at : at + 128] = got_pts[t, 64:128, :]
            value_rows[b, 0:64, at : at + 128] = got_pts[t, 128:192, :]
            key_grad[b, at : at + 128, :] = jnp.transpose(got_pts[t, 0:128, :])
            value_cols[b, at : at + 128, 0:64] = jnp.transpose(got_pts[t, 128:192, :])
            value_cols[b, at : at + 128, 64:128] = jnp.zeros((128, 64), BF16)

        loop(1, SLOTS, lambda k: all_copy(lat, s_all, r_all, member, (member + k) % SLOTS).wait_recv())

        left = iota((CROWS, 128), 1) < HEAD_DIM

        def chunk_of(order):
            cc = (1 - c) if order < 2 else c
            far = order % 2 == 0
            zc = (1 - z // 4) if far else z // 4
            return cc, zc, cc * 2 + zc

        def core_copy(src, dst, s, r, cc, zc, order):
            g = cc * 8 + zc * 4
            return remote(
                src.at[pl.ds(g, CHUNK)], dst.at[pl.ds(zc * 4, CHUNK)], s.at[order], r.at[zc],
                in_column((1 - c) * 8 + z),
            )

        def z_copy(src, dst, s, r, z_to, z_from):
            return remote(src.at[z_to], dst.at[z_from], s.at[z_to], r.at[z_from], in_column(c * 8 + z_to))

        def scatter(order, part, core_got, total, z_got, s1, r1, s2, r2):
            cc, zc, _ = chunk_of(order)
            if order < 2:
                core_copy(part, core_got, s1, r1, cc, zc, order).start()
                return
            core_copy(part, core_got, s1, r1, cc, zc, order % 2).wait_recv()

            def send(i):
                zz = zc * 4 + i
                total[zz] = part[c * 8 + zz] + core_got[zz]

                @pl.when(zz != z)
                def _():
                    z_copy(total, z_got, s2, r2, zz, z).start()

                @pl.when(zz == z)
                def _():
                    z_got[z] = total[z]

            loop(0, CHUNK, send)

        def scatter_wait(z_got, total, s2, r2):
            loop(1, 8, lambda k: z_copy(total, z_got, s2, r2, z, (z + k) % 8).wait_recv())
            result = z_got[0]
            for i in range(1, 8):
                result = result + z_got[i]
            return result

        for order in range(4):
            cc, zc, ch = chunk_of(order)
            lat_c = lat[pl.ds(ch * CHUNK, CHUNK)].reshape(CROWS, 128)
            lat_turned[ch] = jnp.transpose(lat_c)[0:64]

            def block(b, accs):
                mix_acc, u_acc = accs
                scores = dot(lat[pl.ds(ch * CHUNK, CHUNK)].reshape(CROWS, 128), key_rows[b])
                d = jnp.exp(scores - dnorm[b, 0:1, :])
                e = jnp.exp(scores - enorm[pl.ds(ch * CHUNK, CHUNK)].reshape(CROWS, 128)[:, 0:1])
                dec[ch, b] = d
                enc[ch, b] = e
                mix_acc = mix_acc + dot(d.astype(BF16), key_grad[b])
                u_acc = u_acc + dot(e.astype(BF16), value_cols[b])
                return mix_acc, u_acc

            blank = jnp.zeros((CROWS, 128), F32)
            mix_acc, u_acc = lax.fori_loop(0, NB, block, (blank, blank))
            mixu[pl.ds(ch * CHUNK, CHUNK)] = jnp.where(left, u_acc, mix_acc).reshape(CHUNK, BLOCK, 128)
            scatter(order, mixu, from_core, summed, from_z, s_core, r_core, s_z, r_z)

        query_acc[...] = jnp.zeros((4, CROWS, 128), F32)

        def decoder_block(b):
            def totals(ch, total):
                dg = dot(lat[pl.ds(ch * CHUNK, CHUNK)].reshape(CROWS, 128), grad_rows[b])
                dgrad[ch] = dg
                return total + jnp.sum(dec[ch, b] * dg, axis=0, keepdims=True)

            row_total = lax.fori_loop(0, 4, totals, jnp.zeros((1, NW), F32))

            def grads(ch, acc):
                ds = (dec[ch, b] * (dgrad[ch] - row_total)).astype(BF16)
                query_acc[ch] = query_acc[ch] + dot(ds, key_grad[b])
                return acc + dot(lat_turned[ch], ds)

            keys_t[b] = lax.fori_loop(0, 4, grads, jnp.zeros((64, NW), F32))
            values_t[b] = jnp.zeros((64, NW), F32)

        loop(0, 1, decoder_block)

        own = scatter_wait(from_z, summed, s_z, r_z)
        lane = iota((BLOCK, 128), 1)
        mix_half = pltpu.roll(own, HEAD_DIM, 1).astype(BF16).astype(F32)
        column_total = jnp.sum(jnp.where(lane < HEAD_DIM, own * mix_half, 0.0), axis=1, keepdims=True)
        one, two, three = three_terms(column_total)
        mix_all[member] = jnp.where(
            lane < HEAD_DIM, mix_half,
            jnp.where(lane == 64, one, jnp.where(lane == 65, two, jnp.where(lane == 66, three, 0.0))),
        ).astype(BF16)
        loop(1, SLOTS, lambda k: all_copy(mix_all, s_mix, r_mix, (member + k) % SLOTS, member).start())

        loop(1, NB, decoder_block)

        loop(1, SLOTS, lambda k: all_copy(mix_all, s_mix, r_mix, member, (member + k) % SLOTS).wait_recv())

        for order in range(4):
            cc, zc, ch = chunk_of(order)
            mix_turned = jnp.transpose(mix_all[pl.ds(ch * CHUNK, CHUNK)].reshape(CROWS, 128))[0:64]

            def block2(b, acc):
                eg = dot(mix_all[pl.ds(ch * CHUNK, CHUNK)].reshape(CROWS, 128), value_rows[b])
                e = enc[ch, b]
                ds = (e * eg).astype(BF16)
                values_t[b] = values_t[b] + dot(mix_turned, e.astype(BF16))
                keys_t[b] = keys_t[b] + dot(lat_turned[ch], ds)
                return acc + dot(ds, key_grad[b])

            acc = lax.fori_loop(0, NB, block2, query_acc[ch]) * 0.125
            acc = acc.reshape(CHUNK, BLOCK, 128)
            upper = acc[:, 0:32, :].reshape(CHUNK * 32, 128)
            lower = pltpu.roll(acc[:, 32:64, :].reshape(CHUNK * 32, 128), HEAD_DIM, 1)
            packed = jnp.where(iota((CHUNK * 32, 128), 1) < HEAD_DIM, upper, lower)
            lg_part[pl.ds(ch * CHUNK, CHUNK)] = packed.reshape(CHUNK, 32, 128)
            scatter(order, lg_part, lg_core, lg_summed, lg_z, s_core2, r_core2, s_z2, r_z2)

        for t in range(SLOTS):
            b, at = t // 4, 128 * (t % 4)
            kv_send[t, 0:64, :] = keys_t[b, :, at : at + 128].astype(BF16)
            kv_send[t, 64:128, :] = values_t[b, :, at : at + 128].astype(BF16)

    def kv_copy(t, h):
        return remote(kv_send.at[t], kv_got.at[h], s_kv.at[t], r_kv.at[h], in_plane(t))

    def lg_copy(t, h):
        row = ((t // 4) % 2) * 16 + ((t % 4) // 2) * 8
        return remote(lg_own.at[pl.ds(row, 8)], lg_got.at[h], s_lg.at[t], r_lg.at[h], in_plane(t))

    @pl.when(slot < HEADS)
    def _():
        loop(1, SLOTS, lambda k: kv_copy((slot + k) % SLOTS, slot).start())
        kv_got[slot] = kv_send[slot]

        def z_copy2(z_to, z_from):
            return remote(
                lg_summed.at[z_to], lg_z.at[z_from], s_z2.at[z_to], r_z2.at[z_from], in_column(c * 8 + z_to)
            )

        loop(1, 8, lambda k: z_copy2(z, (z + k) % 8).wait_recv())
        result = lg_z[0]
        for i in range(1, 8):
            result = result + lg_z[i]
        lg_own[...] = result
        loop(1, SLOTS, lambda k: lg_copy((slot + k) % SLOTS, slot).start())
        row = pl.multiple_of((x % 2) * 16 + (y // 2) * 8, 8)
        lg_got[slot] = lg_own[pl.ds(row, 8), :]

    def from_heads(copy):
        def body(k):
            h = (slot + k) % SLOTS

            @pl.when(h < HEADS)
            def _():
                copy(slot, h).wait_recv()

        loop(1, SLOTS, body)

    from_heads(kv_copy)
    for p in range(HEADS // 2):
        for i, ref in enumerate((kout_ref, vout_ref)):
            both = jnp.concatenate(
                [kv_got[2 * p, 64 * i : 64 * i + 64, :], kv_got[2 * p + 1, 64 * i : 64 * i + 64, :]], axis=0
            )
            ref[:, 128 * p : 128 * p + 128] = jnp.transpose(both)

    from_heads(lg_copy)
    left8 = iota((8, 128), 1) < HEAD_DIM
    high = x // 2 == 1
    for p in range(HEADS // 2):
        a, b = lg_got[2 * p], lg_got[2 * p + 1]
        a = jnp.where(high, pltpu.roll(a, HEAD_DIM, 1), a)
        b = jnp.where(high, b, pltpu.roll(b, HEAD_DIM, 1))
        both = jnp.where(left8, a, b)
        lgout_ref[:, 128 * p : 128 * p + 128] = jnp.where(y % 2 == 0, both[0:4], both[4:8])

    def sent(k):
        h = (slot + k) % SLOTS

        @pl.when(h < HEADS)
        def _():
            lat_copy(h, slot).wait_send()
            pts_copy(h, slot).wait_send()

    loop(1, SLOTS, sent)

    @pl.when(slot < HEADS)
    def _():
        def sent_column(k):
            g = (member + k) % SLOTS
            remote(lat.at[member], lat.at[member], s_all.at[g], r_all.at[member], in_column(g)).wait_send()
            remote(mix_all.at[member], mix_all.at[member], s_mix.at[g], r_mix.at[member], in_column(g)).wait_send()
            t = (slot + k) % SLOTS
            kv_copy(t, slot).wait_send()
            lg_copy(t, slot).wait_send()

        loop(1, SLOTS, sent_column)

        def sent_z(k):
            zz = (z + k) % 8
            remote(summed.at[zz], from_z.at[z], s_z.at[zz], r_z.at[z], in_column(c * 8 + zz)).wait_send()
            remote(lg_summed.at[zz], lg_z.at[z], s_z2.at[zz], r_z2.at[z], in_column(c * 8 + zz)).wait_send()

        loop(1, 8, sent_z)
        sibling = in_column((1 - c) * 8 + z)
        for order in range(2):
            zc = (1 - z // 4) if order == 0 else z // 4
            g = (1 - c) * 8 + zc * 4
            remote(
                mixu.at[pl.ds(g, CHUNK)], from_core.at[pl.ds(zc * 4, CHUNK)], s_core.at[order], r_core.at[zc], sibling
            ).wait_send()
            remote(
                lg_part.at[pl.ds(g, CHUNK)], lg_core.at[pl.ds(zc * 4, CHUNK)], s_core2.at[order], r_core2.at[zc], sibling
            ).wait_send()


def shards(point_keys, point_values, out_grad, decoder_norm, latent_query, latent_out, encoder_norm):
    vmem = pl.BlockSpec(memory_space=pltpu.VMEM)
    sem = pltpu.SemaphoreType.DMA
    scratch = [
        pltpu.VMEM((HEADS, 32, 128), BF16),
        pltpu.VMEM((HEADS, 192, 128), BF16),
        pltpu.VMEM((2, 16, 768), F32),
        pltpu.VMEM((SLOTS, 32, 128), BF16),
        pltpu.VMEM((SLOTS, 192, 128), BF16),
        pltpu.VMEM((NB, 128, NW), BF16),
        pltpu.VMEM((NB, 128, NW), BF16),
        pltpu.VMEM((NB, 128, NW), BF16),
        pltpu.VMEM((NB, NW, 128), BF16),
        pltpu.VMEM((NB, NW, 128), BF16),
        pltpu.VMEM((NB, 8, NW), F32),
        pltpu.VMEM((SLOTS, BLOCK, 128), F32),
        pltpu.VMEM((SLOTS, BLOCK, 128), BF16),
        pltpu.VMEM((4, 64, CROWS), BF16),
        pltpu.VMEM((4, NB, CROWS, NW), F32),
        pltpu.VMEM((4, NB, CROWS, NW), F32),
        pltpu.VMEM((4, CROWS, NW), F32),
        pltpu.VMEM((4, CROWS, 128), F32),
        pltpu.VMEM((SLOTS, BLOCK, 128), F32),
        pltpu.VMEM((8, BLOCK, 128), F32),
        pltpu.VMEM((8, BLOCK, 128), F32),
        pltpu.VMEM((8, BLOCK, 128), F32),
        pltpu.VMEM((SLOTS, BLOCK, 128), BF16),
        pltpu.VMEM((NB, 64, NW), F32),
        pltpu.VMEM((NB, 64, NW), F32),
        pltpu.VMEM((SLOTS, 32, 128), F32),
        pltpu.VMEM((8, 32, 128), F32),
        pltpu.VMEM((8, 32, 128), F32),
        pltpu.VMEM((8, 32, 128), F32),
        pltpu.VMEM((32, 128), F32),
        pltpu.VMEM((SLOTS, 128, 128), BF16),
        pltpu.VMEM((HEADS, 128, 128), BF16),
        pltpu.VMEM((HEADS, 8, 128), F32),
        sem((SLOTS,)), sem((SLOTS,)), sem((SLOTS,)), sem((SLOTS,)),
        sem((SLOTS,)), sem((SLOTS,)), sem((2,)), sem((2,)), sem((8,)), sem((8,)),
        sem((SLOTS,)), sem((SLOTS,)), sem((2,)), sem((2,)), sem((8,)), sem((8,)),
        sem((SLOTS,)), sem((SLOTS,)), sem((SLOTS,)), sem((SLOTS,)),
    ]
    return pl.pallas_call(
        kernel,
        out_shape=(
            jax.ShapeDtypeStruct(point_keys.shape, BF16),
            jax.ShapeDtypeStruct(point_values.shape, BF16),
            jax.ShapeDtypeStruct(latent_query.shape, F32),
        ),
        in_specs=[vmem] * 7,
        out_specs=(vmem, vmem, vmem),
        scratch_shapes=scratch,
        compiler_params=pltpu.CompilerParams(
            collective_id=0, has_side_effects=True, vmem_limit_bytes=48 * 1024 * 1024
        ),
        name="routing_backward",
    )(point_keys, point_values, out_grad, decoder_norm, latent_query, latent_out, encoder_norm)


def solution(mesh):
    both = ("pa", "pb")
    rows = P(both, None)
    return jax.shard_map(
        shards,
        mesh=mesh,
        in_specs=(rows, rows, rows, P(None, both), rows, rows, P()),
        out_specs=(rows, rows, rows),
        check_vma=False,
    )
```

```python
import jax
import jax.numpy as jnp
from jax import lax
from jax.experimental import pallas as pl
from jax.experimental.pallas import tpu as pltpu
from jax.sharding import PartitionSpec as P

HEADS = 12
HEAD_DIM = 64
SLOTS = 16
PTS = 128
BLOCK = 64
CHUNK = 4
CROWS = CHUNK * BLOCK
NB = 4
NW = 512
Z_ORDER = (4, 3, 5, 2, 6, 1, 7)
PLANE_ORDER = (10, 9, 11, 6, 14, 5, 7, 13, 15, 2, 8, 1, 3, 4, 12)
MESH = pl.DeviceIdType.MESH
F32 = jnp.float32
BF16 = jnp.bfloat16


def dot(a, b):
    return jnp.dot(a, b, preferred_element_type=F32)


def dot_lanes(a, b):
    return lax.dot_general(a, b, (((1,), (1,)), ((), ())), preferred_element_type=F32)


def three_terms(v):
    one = v.astype(BF16).astype(F32)
    two = (v - one).astype(BF16).astype(F32)
    three = (v - one - two).astype(BF16).astype(F32)
    return one, two, three


def iota(shape, dim):
    return lax.broadcasted_iota(jnp.int32, shape, dim)


def head_at(place):
    x, lane = place // 4, (place // 4 + place % 4) % 4
    return jnp.where(lane < 3, 3 * x + lane, HEADS + x)


def kernel(
    keys_hbm, values_hbm, grad_hbm, dnorm_hbm, query_hbm, lout_hbm, enorm_hbm,
    kv_out, lg_out,
    keys_ref, values_ref, grad_ref, dnorm_ref, query_ref, lout_ref, enorm_ref, s_in,
    send_lat, send_pts, tall, got_lat, got_pts,
    dnorm, enorm,
    lat, lat_turned, dec, enc, dgrad, query_acc,
    mixu, from_core, summed, from_z, mix_all, keys_t, values_t,
    lg_part, lg_core, lg_summed, lg_z, lg_own, kv_send, kv_got, lg_got,
    s_lat, r_lat, s_pts, r_pts, s_all, r_all, s_core, r_core, s_z, r_z,
    s_mix, r_mix, s_core2, r_core2, s_z2, r_z2, s_kv, r_kv, s_lg, r_lg,
):
    inputs = [
        pltpu.make_async_copy(src, dst, s_in.at[i])
        for i, (src, dst) in enumerate((
            (query_hbm, query_ref), (lout_hbm, lout_ref), (dnorm_hbm, dnorm_ref), (keys_hbm, keys_ref),
            (grad_hbm, grad_ref), (values_hbm, values_ref), (enorm_hbm, enorm_ref),
        ))
    ]
    for copy in inputs:
        copy.start()
    pa, pb = lax.axis_index("pa"), lax.axis_index("pb")
    x, zlo, c = pa // 4, (pa // 2) % 2, pa % 2
    y, zhi = pb // 4, pb % 4
    z = zhi * 2 + zlo
    place = x * 4 + y
    head = head_at(place)
    member = c * 8 + z

    def in_plane(t):
        return ((t // 4) * 4 + zlo * 2 + c, (t % 4) * 4 + zhi)

    def in_column(g):
        cc, zz = g // 8, g % 8
        return (x * 4 + (zz % 2) * 2 + cc, y * 4 + zz // 2)

    def plane_at(k):
        return ((x + k // 4) % 4) * 4 + (y + k % 4) % 4

    def remote(src, dst, s, r, to):
        return pltpu.make_async_remote_copy(
            src_ref=src, dst_ref=dst, send_sem=s, recv_sem=r, device_id=to, device_id_type=MESH
        )

    def loop(lo, hi, body):
        def step(i, carry):
            body(i)
            return carry

        lax.fori_loop(lo, hi, step, 0)

    def along_z(buf, s, r, zz):
        return remote(buf.at[member], buf.at[member], s.at[zz], r.at[member], in_column(c * 8 + zz))

    def to_sibling(buf, s, r, zz):
        g = c * 8 + zz
        return remote(buf.at[g], buf.at[g], s.at[8 + zz], r.at[g], in_column((1 - c) * 8 + z))

    def arrival(buf, s, r, g):
        return remote(buf.at[g], buf.at[g], s.at[0], r.at[g], in_column((1 - c) * 8 + z))

    def gather_send(buf, s, r):
        for k in Z_ORDER:
            along_z(buf, s, r, (z + k) % 8).start()
        to_sibling(buf, s, r, z).start()

    def gather_relay(buf, s, r):
        for k in reversed(Z_ORDER):
            zz = (z + k) % 8
            arrival(buf, s, r, c * 8 + zz).wait_recv()
            to_sibling(buf, s, r, zz).start()

    def gather_sibling(buf, s, r, zc):
        for i in range(CHUNK):
            arrival(buf, s, r, (1 - c) * 8 + zc * 4 + i).wait_recv()

    barrier = pltpu.get_barrier_semaphore()

    def greet(k):
        pl.semaphore_signal(barrier, inc=1, device_id=in_plane((place + k) % SLOTS), device_id_type=MESH)
        pl.semaphore_signal(barrier, inc=1, device_id=in_column((member + k) % SLOTS), device_id_type=MESH)

    loop(1, SLOTS, greet)

    for copy in inputs[:3]:
        copy.wait()
    for k in range(4):
        tall[0, 4 * k : 4 * k + 4, :] = query_ref[...].astype(F32) * 0.125
        tall[1, 4 * k : 4 * k + 4, :] = lout_ref[...].astype(F32)
    rows16 = iota((16, 128), 0)
    left16 = iota((16, 128), 1) < HEAD_DIM
    mine = rows16 // 4 == y
    for p in range(HEADS // 2):
        q = tall[0, :, 128 * p : 128 * p + 128]
        o = tall[1, :, 128 * p : 128 * p + 128]
        even = jnp.where(left16, q, pltpu.roll(o, HEAD_DIM, 1))
        odd = jnp.where(left16, pltpu.roll(q, HEAD_DIM, 1), o)
        send_lat[2 * p] = jnp.where(mine, even, 0.0).astype(BF16)
        send_lat[2 * p + 1] = jnp.where(mine, odd, 0.0).astype(BF16)
    for h in range(HEADS):
        one, two, three = three_terms(dnorm_ref[h : h + 1, :])
        send_pts[h, 0:16, :] = jnp.where(
            rows16 == 0, one, jnp.where(rows16 == 1, two, jnp.where(rows16 == 2, three, 0.0))
        ).astype(BF16)

    for copy in inputs[3:]:
        copy.wait()
    for p in range(HEADS // 2):
        for i, ref in enumerate((keys_ref, grad_ref, values_ref)):
            turned = jnp.transpose(ref[:, 128 * p : 128 * p + 128])
            send_pts[2 * p, 64 * i + 16 : 64 * i + 80, :] = turned[0:64]
            send_pts[2 * p + 1, 64 * i + 16 : 64 * i + 80, :] = turned[64:128]

    pl.semaphore_wait(barrier, 2 * (SLOTS - 1))

    def lat_copy(to, src):
        h = head_at(to)
        return remote(send_lat.at[h], got_lat.at[src], s_lat.at[h], r_lat.at[src], in_plane(to))

    def pts_copy(to, src):
        h = head_at(to)
        return remote(send_pts.at[h], got_pts.at[src, pl.ds(0, 208)], s_pts.at[h], r_pts.at[src], in_plane(to))

    def to_heads(copy, order=PLANE_ORDER):
        for k in order:
            to = plane_at(k)

            @pl.when(head_at(to) < HEADS)
            def _():
                copy(to, place).start()

    to_heads(lat_copy)
    to_heads(pts_copy, PLANE_ORDER[:1])

    @pl.when(head >= HEADS)
    def _():
        to_heads(pts_copy, PLANE_ORDER[1:])

    @pl.when(head < HEADS)
    def _():
        got_lat[place] = send_lat[head]
        got_pts[place, 0:208, :] = send_pts[head]

        norm_row = enorm_ref[pl.ds(head, 1), :]
        terms = three_terms(norm_row)

        def norm_block(g):
            cc, zz = g // 8, g % 8
            r = iota((BLOCK, 1024), 0)
            place = (r // 16) * 256 + (zz % 2) * 128 + cc * 64 + ((r // 4) % 4) * 16 + (zz // 2) * 4 + r % 4
            hot = jnp.where(iota((BLOCK, 1024), 1) == place, 1.0, 0.0).astype(BF16)
            total = jnp.zeros((BLOCK, 128), F32)
            for t in terms:
                wide = jnp.broadcast_to(t, (128, 1024)).astype(BF16)
                total = total + lax.dot_general(
                    hot, wide, (((1,), (1,)), ((), ())), preferred_element_type=F32
                )
            enorm[g] = total


        ones_rows = jnp.where(iota((HEAD_DIM, 128), 0) < 3, -1.0, 0.0).astype(BF16)
        for t in range(SLOTS):
            got_pts[t, 208:272, :] = ones_rows

        def lat_wait(k):
            src = (place + k) % SLOTS
            remote(send_lat.at[0], got_lat.at[src], s_lat.at[0], r_lat.at[src], in_plane(src)).wait_recv()

        loop(1, SLOTS, lat_wait)

        for i in range(4):
            total = got_lat[4 * i].astype(F32)
            for j in range(1, 4):
                total = total + got_lat[4 * i + j].astype(F32)
            lat[member, 16 * i : 16 * i + 16, :] = total.astype(BF16)

        gather_send(lat, s_all, r_all)
        to_heads(pts_copy, PLANE_ORDER[1:])
        loop(0, SLOTS, norm_block)

        gather_relay(lat, s_all, r_all)

        def pts_wait(k):
            src = (place + k) % SLOTS
            remote(
                send_pts.at[0], got_pts.at[src, pl.ds(0, 208)], s_pts.at[0], r_pts.at[src], in_plane(src)
            ).wait_recv()

        loop(1, SLOTS, pts_wait)

        for t in range(SLOTS):
            dn = jnp.sum(got_pts[t, 0:16, :].astype(F32), axis=0, keepdims=True)
            dnorm[t // 4, :, 128 * (t % 4) : 128 * (t % 4) + 128] = jnp.broadcast_to(dn, (8, 128))

        left = iota((CROWS, 128), 1) < HEAD_DIM

        lane_c = iota((CROWS, 128), 1)

        def wide(lo, hi, b):
            return jnp.concatenate([got_pts[4 * b + i, lo:hi, :] for i in range(4)], axis=1)

        def queries(ch):
            both = lat[pl.ds(ch * CHUNK, CHUNK)].reshape(CROWS, 128)
            return jnp.where(lane_c < HEAD_DIM, both, jnp.zeros_like(both))

        def outs(ch):
            both = lat[pl.ds(ch * CHUNK, CHUNK)].reshape(CROWS, 128)
            return jnp.where(lane_c < HEAD_DIM, jnp.zeros_like(both), both)

        def chunk_of(order):
            cc = c if order in (0, 3) else 1 - c
            zc = 1 - z // 4 if order < 2 else z // 4
            return cc, zc, cc * 2 + zc

        def core_copy(src, dst, s, r, cc, zc, order):
            g = cc * 8 + zc * 4
            return remote(
                src.at[pl.ds(g, CHUNK)], dst.at[pl.ds(zc * 4, CHUNK)], s.at[order], r.at[zc],
                in_column((1 - c) * 8 + z),
            )

        def z_copy(src, dst, s, r, z_to, z_from):
            return remote(src.at[z_to], dst.at[z_from], s.at[z_to], r.at[z_from], in_column(c * 8 + z_to))

        def scatter(order, part, core_got, total, z_got, s1, r1, s2, r2):
            if order == 0:
                return
            if order < 3:
                cc, zc, _ = chunk_of(order)
                core_copy(part, core_got, s1, r1, cc, zc, order - 1).start()
                if order == 1:
                    return
            cc, zc, _ = chunk_of(0 if order == 2 else 3)
            core_copy(part, core_got, s1, r1, cc, zc, 0).wait_recv()

            def send(i):
                zz = zc * 4 + i
                total[zz] = part[c * 8 + zz] + core_got[zz]

                @pl.when(zz != z)
                def _():
                    z_copy(total, z_got, s2, r2, zz, z).start()

                @pl.when(zz == z)
                def _():
                    z_got[z] = total[z]

            loop(0, CHUNK, send)

        def scatter_wait(z_got, total, s2, r2):
            loop(1, 8, lambda k: z_copy(total, z_got, s2, r2, z, (z + k) % 8).wait_recv())
            result = z_got[0]
            for i in range(1, 8):
                result = result + z_got[i]
            return result

        for order in range(4):
            cc, zc, ch = chunk_of(order)
            if order in (1, 2):
                gather_sibling(lat, s_all, r_all, zc)
            lat_c = lat[pl.ds(ch * CHUNK, CHUNK)].reshape(CROWS, 128)
            lat_turned[ch] = jnp.transpose(lat_c)[0:64]

            def block(b, accs):
                mix_acc, u_acc = accs
                keys_grads = wide(16, 144, b)
                scores = dot(queries(ch), keys_grads)
                d = jnp.exp(scores - dnorm[b, 0:1, :])
                e = jnp.exp(scores - enorm[pl.ds(ch * CHUNK, CHUNK)].reshape(CROWS, 128)[:, 0:1])
                dec[ch, b] = d
                enc[ch, b] = e
                mix_acc = mix_acc + dot_lanes(d.astype(BF16), keys_grads)
                u_acc = u_acc + dot_lanes(e.astype(BF16), wide(144, 272, b))
                return mix_acc, u_acc

            blank = jnp.zeros((CROWS, 128), F32)
            mix_acc, u_acc = lax.fori_loop(0, NB, block, (blank, blank))
            mixu[pl.ds(ch * CHUNK, CHUNK)] = jnp.where(left, u_acc, mix_acc).reshape(CHUNK, BLOCK, 128)
            scatter(order, mixu, from_core, summed, from_z, s_core, r_core, s_z, r_z)

        query_acc[...] = jnp.zeros((4, CROWS, 128), F32)

        def decoder_block(b):
            def totals(ch, total):
                dg = dot(outs(ch), wide(16, 144, b))
                dgrad[ch] = dg
                return total + jnp.sum(dec[ch, b] * dg, axis=0, keepdims=True)

            row_total = lax.fori_loop(0, 4, totals, jnp.zeros((1, NW), F32))

            def grads(ch, acc):
                ds = (dec[ch, b] * (dgrad[ch] - row_total)).astype(BF16)
                query_acc[ch] = query_acc[ch] + dot_lanes(ds, wide(16, 144, b))
                return acc + dot(lat_turned[ch], ds)

            keys_t[b] = lax.fori_loop(0, 4, grads, jnp.zeros((64, NW), F32))
            values_t[b] = jnp.zeros((64, NW), F32)

        loop(0, 1, decoder_block)

        own = scatter_wait(from_z, summed, s_z, r_z)
        lane = iota((BLOCK, 128), 1)
        mix_half = pltpu.roll(own, HEAD_DIM, 1).astype(BF16).astype(F32)
        column_total = jnp.sum(jnp.where(lane < HEAD_DIM, own * mix_half, 0.0), axis=1, keepdims=True)
        one, two, three = three_terms(column_total)
        mix_all[member] = jnp.where(
            lane < HEAD_DIM, mix_half,
            jnp.where(lane == 64, one, jnp.where(lane == 65, two, jnp.where(lane == 66, three, 0.0))),
        ).astype(BF16)
        gather_send(mix_all, s_mix, r_mix)

        loop(1, NB, decoder_block)

        gather_relay(mix_all, s_mix, r_mix)

        for order in range(4):
            cc, zc, ch = chunk_of(order)
            if order in (1, 2):
                gather_sibling(mix_all, s_mix, r_mix, zc)
            mix_turned = jnp.transpose(mix_all[pl.ds(ch * CHUNK, CHUNK)].reshape(CROWS, 128))[0:64]

            def block2(b, acc):
                eg = dot(mix_all[pl.ds(ch * CHUNK, CHUNK)].reshape(CROWS, 128), wide(144, 272, b))
                e = enc[ch, b]
                ds = (e * eg).astype(BF16)
                values_t[b] = values_t[b] + dot(mix_turned, e.astype(BF16))
                keys_t[b] = keys_t[b] + dot(lat_turned[ch], ds)
                return acc + dot_lanes(ds, wide(16, 144, b))

            acc = lax.fori_loop(0, NB, block2, query_acc[ch]) * 0.125
            acc = acc.reshape(CHUNK, BLOCK, 128)
            upper = acc[:, 0:32, :].reshape(CHUNK * 32, 128)
            lower = pltpu.roll(acc[:, 32:64, :].reshape(CHUNK * 32, 128), HEAD_DIM, 1)
            packed = jnp.where(iota((CHUNK * 32, 128), 1) < HEAD_DIM, upper, lower)
            lg_part[pl.ds(ch * CHUNK, CHUNK)] = packed.reshape(CHUNK, 32, 128)
            scatter(order, lg_part, lg_core, lg_summed, lg_z, s_core2, r_core2, s_z2, r_z2)

        for t in range(SLOTS):
            b, at = t // 4, 128 * (t % 4)
            kv_send[t, 0:64, :] = keys_t[b, :, at : at + 128].astype(BF16)
            kv_send[t, 64:128, :] = values_t[b, :, at : at + 128].astype(BF16)

    def kv_copy(t, h):
        return remote(kv_send.at[t], kv_got.at[h], s_kv.at[t], r_kv.at[h], in_plane(t))

    def lg_copy(t, h):
        row = ((t // 4) % 2) * 16 + ((t % 4) // 2) * 8
        return remote(lg_own.at[pl.ds(row, 8)], lg_got.at[h], s_lg.at[t], r_lg.at[h], in_plane(t))

    @pl.when(head < HEADS)
    def _():
        loop(1, SLOTS, lambda k: kv_copy((place + k) % SLOTS, head).start())
        kv_got[head] = kv_send[place]

        def z_copy2(z_to, z_from):
            return remote(
                lg_summed.at[z_to], lg_z.at[z_from], s_z2.at[z_to], r_z2.at[z_from], in_column(c * 8 + z_to)
            )

        loop(1, 8, lambda k: z_copy2(z, (z + k) % 8).wait_recv())
        result = lg_z[0]
        for i in range(1, 8):
            result = result + lg_z[i]
        lg_own[...] = result
        for k in PLANE_ORDER:
            lg_copy(plane_at(k), head).start()
        row = pl.multiple_of((x % 2) * 16 + (y // 2) * 8, 8)
        lg_got[head] = lg_own[pl.ds(row, 8), :]

    def from_heads(copy):
        def body(k):
            src = (place + k) % SLOTS

            @pl.when(head_at(src) < HEADS)
            def _():
                copy(place, head_at(src)).wait_recv()

        loop(1, SLOTS, body)

    from_heads(kv_copy)
    kv_out[...] = kv_got[...]
    from_heads(lg_copy)
    lg_out[...] = lg_got[...]

    def sent(k):
        to = (place + k) % SLOTS

        @pl.when(head_at(to) < HEADS)
        def _():
            lat_copy(to, place).wait_send()
            pts_copy(to, place).wait_send()

    loop(1, SLOTS, sent)

    @pl.when(head < HEADS)
    def _():
        def sent_column(k):
            t = (place + k) % SLOTS
            kv_copy(t, head).wait_send()
            lg_copy(t, head).wait_send()

        loop(1, SLOTS, sent_column)
        to_sibling(lat, s_all, r_all, z).wait_send()
        to_sibling(mix_all, s_mix, r_mix, z).wait_send()

        def sent_z(k):
            zz = (z + k) % 8
            for buf, s, r in ((lat, s_all, r_all), (mix_all, s_mix, r_mix)):
                along_z(buf, s, r, zz).wait_send()
                to_sibling(buf, s, r, zz).wait_send()
            remote(summed.at[zz], from_z.at[z], s_z.at[zz], r_z.at[z], in_column(c * 8 + zz)).wait_send()
            remote(lg_summed.at[zz], lg_z.at[z], s_z2.at[zz], r_z2.at[z], in_column(c * 8 + zz)).wait_send()

        loop(1, 8, sent_z)
        sibling = in_column((1 - c) * 8 + z)
        for order in range(2):
            zc = (1 - z // 4) if order == 0 else z // 4
            g = (1 - c) * 8 + zc * 4
            remote(
                mixu.at[pl.ds(g, CHUNK)], from_core.at[pl.ds(zc * 4, CHUNK)], s_core.at[order], r_core.at[zc], sibling
            ).wait_send()
            remote(
                lg_part.at[pl.ds(g, CHUNK)], lg_core.at[pl.ds(zc * 4, CHUNK)], s_core2.at[order], r_core2.at[zc], sibling
            ).wait_send()


def unpack(kv_ref, lg_ref, kout_ref, vout_ref, lgout_ref):
    pa, pb = lax.axis_index("pa"), lax.axis_index("pb")
    high, y = pa // 8 == 1, pb // 4
    for p in range(HEADS // 2):
        for i, ref in enumerate((kout_ref, vout_ref)):
            both = jnp.concatenate(
                [kv_ref[2 * p, 64 * i : 64 * i + 64, :], kv_ref[2 * p + 1, 64 * i : 64 * i + 64, :]], axis=0
            )
            ref[:, 128 * p : 128 * p + 128] = jnp.transpose(both)
    left8 = iota((8, 128), 1) < HEAD_DIM
    for p in range(HEADS // 2):
        a, b = lg_ref[2 * p], lg_ref[2 * p + 1]
        a = jnp.where(high, pltpu.roll(a, HEAD_DIM, 1), a)
        b = jnp.where(high, b, pltpu.roll(b, HEAD_DIM, 1))
        both = jnp.where(left8, a, b)
        lgout_ref[:, 128 * p : 128 * p + 128] = jnp.where(y % 2 == 0, both[0:4], both[4:8])


def shards(point_keys, point_values, out_grad, decoder_norm, latent_query, latent_out, encoder_norm):
    vmem = pl.BlockSpec(memory_space=pltpu.VMEM)
    sem = pltpu.SemaphoreType.DMA
    scratch = [
        pltpu.VMEM((PTS, 768), BF16), pltpu.VMEM((PTS, 768), BF16), pltpu.VMEM((PTS, 768), BF16),
        pltpu.VMEM((HEADS, PTS), F32), pltpu.VMEM((4, 768), BF16), pltpu.VMEM((4, 768), BF16),
        pltpu.VMEM((HEADS, 1024), F32), sem((7,)),
        pltpu.VMEM((HEADS, 16, 128), BF16),
        pltpu.VMEM((HEADS, 208, 128), BF16),
        pltpu.VMEM((2, 16, 768), F32),
        pltpu.VMEM((SLOTS, 16, 128), BF16),
        pltpu.VMEM((SLOTS, 272, 128), BF16),
        pltpu.VMEM((NB, 8, NW), F32),
        pltpu.VMEM((SLOTS, BLOCK, 128), F32),
        pltpu.VMEM((SLOTS, BLOCK, 128), BF16),
        pltpu.VMEM((4, 64, CROWS), BF16),
        pltpu.VMEM((4, NB, CROWS, NW), F32),
        pltpu.VMEM((4, NB, CROWS, NW), F32),
        pltpu.VMEM((4, CROWS, NW), F32),
        pltpu.VMEM((4, CROWS, 128), F32),
        pltpu.VMEM((SLOTS, BLOCK, 128), F32),
        pltpu.VMEM((8, BLOCK, 128), F32),
        pltpu.VMEM((8, BLOCK, 128), F32),
        pltpu.VMEM((8, BLOCK, 128), F32),
        pltpu.VMEM((SLOTS, BLOCK, 128), BF16),
        pltpu.VMEM((NB, 64, NW), F32),
        pltpu.VMEM((NB, 64, NW), F32),
        pltpu.VMEM((SLOTS, 32, 128), F32),
        pltpu.VMEM((8, 32, 128), F32),
        pltpu.VMEM((8, 32, 128), F32),
        pltpu.VMEM((8, 32, 128), F32),
        pltpu.VMEM((32, 128), F32),
        pltpu.VMEM((SLOTS, 128, 128), BF16),
        pltpu.VMEM((HEADS, 128, 128), BF16),
        pltpu.VMEM((HEADS, 8, 128), F32),
        sem((SLOTS,)), sem((SLOTS,)), sem((SLOTS,)), sem((SLOTS,)),
        sem((SLOTS,)), sem((SLOTS,)), sem((2,)), sem((2,)), sem((8,)), sem((8,)),
        sem((SLOTS,)), sem((SLOTS,)), sem((2,)), sem((2,)), sem((8,)), sem((8,)),
        sem((SLOTS,)), sem((SLOTS,)), sem((SLOTS,)), sem((SLOTS,)),
    ]
    kv, lg = pl.pallas_call(
        kernel,
        out_shape=(
            pltpu.VMEM((HEADS, 128, 128), BF16),
            pltpu.VMEM((HEADS, 8, 128), F32),
        ),
        in_specs=[pl.BlockSpec(memory_space=pl.ANY)] * 7,
        out_specs=(vmem, vmem),
        scratch_shapes=scratch,
        compiler_params=pltpu.CompilerParams(
            collective_id=0, has_side_effects=True, vmem_limit_bytes=56 * 1024 * 1024
        ),
        name="routing_backward",
    )(point_keys, point_values, out_grad, decoder_norm, latent_query, latent_out, encoder_norm)
    return pl.pallas_call(
        unpack,
        out_shape=(
            jax.ShapeDtypeStruct(point_keys.shape, BF16),
            jax.ShapeDtypeStruct(point_values.shape, BF16),
            jax.ShapeDtypeStruct(latent_query.shape, F32),
        ),
        in_specs=[vmem] * 2,
        out_specs=(vmem, vmem, vmem),
        compiler_params=pltpu.CompilerParams(vmem_limit_bytes=8 * 1024 * 1024),
        name="unpack",
    )(kv, lg)


def solution(mesh):
    both = ("pa", "pb")
    rows = P(both, None)
    return jax.shard_map(
        shards,
        mesh=mesh,
        in_specs=(rows, rows, rows, P(None, both), rows, rows, P()),
        out_specs=(rows, rows, rows),
        check_vma=False,
    )
```

```python
import jax
import jax.numpy as jnp
from jax import lax
from jax.experimental import pallas as pl
from jax.experimental.pallas import tpu as pltpu
from jax.sharding import PartitionSpec as P

HEADS = 12
HEAD_DIM = 64
SLOTS = 16
PTS = 128
BLOCK = 64
CHUNK = 4
CROWS = CHUNK * BLOCK
NB = 1
NW = 2048
Z_ORDER = (4, 3, 5, 2, 6, 1, 7)
PLANE_ORDER = (10, 9, 11, 6, 14, 5, 7, 13, 15, 2, 8, 1, 3, 4, 12)
MESH = pl.DeviceIdType.MESH
F32 = jnp.float32
BF16 = jnp.bfloat16


def dot(a, b):
    return jnp.dot(a, b, preferred_element_type=F32)


def dot_lanes(a, b):
    return lax.dot_general(a, b, (((1,), (1,)), ((), ())), preferred_element_type=F32)


def three_terms(v):
    one = v.astype(BF16).astype(F32)
    two = (v - one).astype(BF16).astype(F32)
    three = (v - one - two).astype(BF16).astype(F32)
    return one, two, three


def iota(shape, dim):
    return lax.broadcasted_iota(jnp.int32, shape, dim)


def head_at(place):
    x, lane = place // 4, (place // 4 + place % 4) % 4
    return jnp.where(lane < 3, 3 * x + lane, HEADS + x)


def kernel(
    keys_hbm, values_hbm, grad_hbm, dnorm_hbm, query_hbm, lout_hbm, enorm_hbm,
    kv_out, lg_out,
    keys_ref, values_ref, grad_ref, dnorm_ref, query_ref, lout_ref, enorm_ref, s_in,
    send_lat, send_pts, tall, got_lat, got_pts,
    dnorm, enorm,
    lat, lat_turned, dec, enc, dgrad, query_acc,
    mixu, from_core, summed, from_z, summed_u, from_z_u, mix_all, keys_t, values_t,
    lg_part, lg_core, lg_summed, lg_z, lg_own, kv_send, kv_got, lg_got,
    s_lat, r_lat, s_pts, r_pts, s_all, r_all, s_core, r_core, s_z, r_z, s_zu, r_zu,
    s_mix, r_mix, s_core2, r_core2, s_z2, r_z2, s_kv, r_kv, s_lg, r_lg,
):
    inputs = [
        pltpu.make_async_copy(src, dst, s_in.at[i])
        for i, (src, dst) in enumerate((
            (query_hbm, query_ref), (lout_hbm, lout_ref), (dnorm_hbm, dnorm_ref), (keys_hbm, keys_ref),
            (grad_hbm, grad_ref), (values_hbm, values_ref), (enorm_hbm, enorm_ref),
        ))
    ]
    for copy in inputs:
        copy.start()
    pa, pb = lax.axis_index("pa"), lax.axis_index("pb")
    x, zlo, c = pa // 4, (pa // 2) % 2, pa % 2
    y, zhi = pb // 4, pb % 4
    z = zhi * 2 + zlo
    place = x * 4 + y
    head = head_at(place)
    member = c * 8 + z

    def in_plane(t):
        return ((t // 4) * 4 + zlo * 2 + c, (t % 4) * 4 + zhi)

    def in_column(g):
        cc, zz = g // 8, g % 8
        return (x * 4 + (zz % 2) * 2 + cc, y * 4 + zz // 2)

    def plane_at(k):
        return ((x + k // 4) % 4) * 4 + (y + k % 4) % 4

    def remote(src, dst, s, r, to):
        return pltpu.make_async_remote_copy(
            src_ref=src, dst_ref=dst, send_sem=s, recv_sem=r, device_id=to, device_id_type=MESH
        )

    def loop(lo, hi, body):
        def step(i, carry):
            body(i)
            return carry

        lax.fori_loop(lo, hi, step, 0)

    def along_z(buf, s, r, zz):
        return remote(buf.at[member], buf.at[member], s.at[zz], r.at[member], in_column(c * 8 + zz))

    def to_sibling(buf, s, r, zz):
        g = c * 8 + zz
        return remote(buf.at[g], buf.at[g], s.at[8 + zz], r.at[g], in_column((1 - c) * 8 + z))

    def arrival(buf, s, r, g):
        return remote(buf.at[g], buf.at[g], s.at[0], r.at[g], in_column((1 - c) * 8 + z))

    def gather_send(buf, s, r):
        for k in Z_ORDER:
            along_z(buf, s, r, (z + k) % 8).start()
        to_sibling(buf, s, r, z).start()

    def gather_relay(buf, s, r):
        for k in reversed(Z_ORDER):
            zz = (z + k) % 8
            arrival(buf, s, r, c * 8 + zz).wait_recv()
            to_sibling(buf, s, r, zz).start()

    def gather_sibling(buf, s, r, zc):
        for i in range(CHUNK):
            arrival(buf, s, r, (1 - c) * 8 + zc * 4 + i).wait_recv()

    barrier = pltpu.get_barrier_semaphore()

    def greet(k):
        pl.semaphore_signal(barrier, inc=1, device_id=in_plane((place + k) % SLOTS), device_id_type=MESH)
        pl.semaphore_signal(barrier, inc=1, device_id=in_column((member + k) % SLOTS), device_id_type=MESH)

    loop(1, SLOTS, greet)

    for copy in inputs[:3]:
        copy.wait()
    for k in range(4):
        tall[0, 4 * k : 4 * k + 4, :] = query_ref[...].astype(F32) * 0.125
        tall[1, 4 * k : 4 * k + 4, :] = lout_ref[...].astype(F32)
    rows16 = iota((16, 128), 0)
    left16 = iota((16, 128), 1) < HEAD_DIM
    mine = rows16 // 4 == y
    for p in range(HEADS // 2):
        q = tall[0, :, 128 * p : 128 * p + 128]
        o = tall[1, :, 128 * p : 128 * p + 128]
        even = jnp.where(left16, q, pltpu.roll(o, HEAD_DIM, 1))
        odd = jnp.where(left16, pltpu.roll(q, HEAD_DIM, 1), o)
        send_lat[2 * p] = jnp.where(mine, even, 0.0).astype(BF16)
        send_lat[2 * p + 1] = jnp.where(mine, odd, 0.0).astype(BF16)
    for h in range(HEADS):
        one, two, three = three_terms(dnorm_ref[h : h + 1, :])
        send_pts[h, 0:16, :] = jnp.where(
            rows16 == 0, one, jnp.where(rows16 == 1, two, jnp.where(rows16 == 2, three, 0.0))
        ).astype(BF16)

    for copy in inputs[3:]:
        copy.wait()
    for p in range(HEADS // 2):
        for i, ref in enumerate((keys_ref, grad_ref, values_ref)):
            turned = jnp.transpose(ref[:, 128 * p : 128 * p + 128])
            send_pts[2 * p, 64 * i + 16 : 64 * i + 80, :] = turned[0:64]
            send_pts[2 * p + 1, 64 * i + 16 : 64 * i + 80, :] = turned[64:128]

    pl.semaphore_wait(barrier, 2 * (SLOTS - 1))

    def lat_copy(to, src):
        h = head_at(to)
        return remote(send_lat.at[h], got_lat.at[src], s_lat.at[h], r_lat.at[src], in_plane(to))

    def pts_copy(to, src):
        h = head_at(to)
        return remote(send_pts.at[h], got_pts.at[src, pl.ds(0, 208)], s_pts.at[h], r_pts.at[src], in_plane(to))

    def to_heads(copy, order=PLANE_ORDER):
        for k in order:
            to = plane_at(k)

            @pl.when(head_at(to) < HEADS)
            def _():
                copy(to, place).start()

    to_heads(lat_copy)
    to_heads(pts_copy, PLANE_ORDER[:1])

    @pl.when(head >= HEADS)
    def _():
        to_heads(pts_copy, PLANE_ORDER[1:])

    @pl.when(head < HEADS)
    def _():
        got_lat[place] = send_lat[head]
        got_pts[place, 0:208, :] = send_pts[head]

        norm_row = enorm_ref[pl.ds(head, 1), :]
        terms = three_terms(norm_row)

        def norm_block(g):
            cc, zz = g // 8, g % 8
            r = iota((BLOCK, 1024), 0)
            place = (r // 16) * 256 + (zz % 2) * 128 + cc * 64 + ((r // 4) % 4) * 16 + (zz // 2) * 4 + r % 4
            hot = jnp.where(iota((BLOCK, 1024), 1) == place, 1.0, 0.0).astype(BF16)
            total = jnp.zeros((BLOCK, 128), F32)
            for t in terms:
                wide = jnp.broadcast_to(t, (128, 1024)).astype(BF16)
                total = total + lax.dot_general(
                    hot, wide, (((1,), (1,)), ((), ())), preferred_element_type=F32
                )
            enorm[g] = total


        ones_rows = jnp.where(iota((HEAD_DIM, 128), 0) < 3, -1.0, 0.0).astype(BF16)
        for t in range(SLOTS):
            got_pts[t, 208:272, :] = ones_rows

        def lat_wait(k):
            src = (place + k) % SLOTS
            remote(send_lat.at[0], got_lat.at[src], s_lat.at[0], r_lat.at[src], in_plane(src)).wait_recv()

        loop(1, SLOTS, lat_wait)

        for i in range(4):
            total = got_lat[4 * i].astype(F32)
            for j in range(1, 4):
                total = total + got_lat[4 * i + j].astype(F32)
            lat[member, 16 * i : 16 * i + 16, :] = total.astype(BF16)

        gather_send(lat, s_all, r_all)
        to_heads(pts_copy, PLANE_ORDER[1:])
        loop(0, SLOTS, norm_block)

        gather_relay(lat, s_all, r_all)

        def pts_wait(k):
            src = (place + k) % SLOTS
            remote(
                send_pts.at[0], got_pts.at[src, pl.ds(0, 208)], s_pts.at[0], r_pts.at[src], in_plane(src)
            ).wait_recv()

        loop(1, SLOTS, pts_wait)

        for t in range(SLOTS):
            dn = jnp.sum(got_pts[t, 0:16, :].astype(F32), axis=0, keepdims=True)
            dnorm[t // 16, :, 128 * (t % 16) : 128 * (t % 16) + 128] = jnp.broadcast_to(dn, (8, 128))

        left = iota((CROWS, 128), 1) < HEAD_DIM

        lane_c = iota((CROWS, 128), 1)

        def wide(lo, hi, b):
            return jnp.concatenate([got_pts[16 * b + i, lo:hi, :] for i in range(16)], axis=1)

        def queries(ch):
            both = lat[pl.ds(ch * CHUNK, CHUNK)].reshape(CROWS, 128)
            return jnp.where(lane_c < HEAD_DIM, both, jnp.zeros_like(both))

        def outs(ch):
            both = lat[pl.ds(ch * CHUNK, CHUNK)].reshape(CROWS, 128)
            return jnp.where(lane_c < HEAD_DIM, jnp.zeros_like(both), both)

        def chunk_of(order):
            cc = c if order in (0, 3) else 1 - c
            zc = 1 - z // 4 if order < 2 else z // 4
            return cc, zc, cc * 2 + zc

        def core_copy(src, dst, s, r, cc, zc, order):
            g = cc * 8 + zc * 4
            return remote(
                src.at[pl.ds(g, CHUNK)], dst.at[pl.ds(zc * 4, CHUNK)], s.at[order], r.at[zc],
                in_column((1 - c) * 8 + z),
            )

        def z_copy(src, dst, s, r, z_to, z_from):
            return remote(src.at[z_to], dst.at[z_from], s.at[z_to], r.at[z_from], in_column(c * 8 + z_to))

        left32 = iota((32, 128), 1) < HEAD_DIM

        def mixu_send(zz):
            both = mixu[c * 8 + zz] + from_core[zz]
            upper, lower = both[0:32], pltpu.roll(both[32:64], HEAD_DIM, 1)
            summed[zz] = jnp.where(left32, lower, upper)
            summed_u[zz] = jnp.where(left32, upper, lower).astype(BF16)

            @pl.when(zz != z)
            def _():
                z_copy(summed, from_z, s_z, r_z, zz, z).start()
                z_copy(summed_u, from_z_u, s_zu, r_zu, zz, z).start()

            @pl.when(zz == z)
            def _():
                from_z[z] = summed[z]
                from_z_u[z] = summed_u[z]

        def scatter(order, part, core_got, total, z_got, s1, r1, s2, r2, send_one=None):
            if order == 0:
                return
            if order < 3:
                cc, zc, _ = chunk_of(order)
                core_copy(part, core_got, s1, r1, cc, zc, order - 1).start()
                if order == 1:
                    return
            cc, zc, _ = chunk_of(0 if order == 2 else 3)
            core_copy(part, core_got, s1, r1, cc, zc, 0).wait_recv()

            def send(i):
                zz = zc * 4 + i
                total[zz] = (part[c * 8 + zz] + core_got[zz]).astype(total.dtype)

                @pl.when(zz != z)
                def _():
                    z_copy(total, z_got, s2, r2, zz, z).start()

                @pl.when(zz == z)
                def _():
                    z_got[z] = total[z]

            loop(0, CHUNK, send if send_one is None else lambda i: send_one(zc * 4 + i))

        def scatter_wait(z_got, total, s2, r2):
            loop(1, 8, lambda k: z_copy(total, z_got, s2, r2, z, (z + k) % 8).wait_recv())
            result = z_got[0].astype(F32)
            for i in range(1, 8):
                result = result + z_got[i].astype(F32)
            return result

        for order in range(4):
            cc, zc, ch = chunk_of(order)
            if order in (1, 2):
                gather_sibling(lat, s_all, r_all, zc)
            lat_c = lat[pl.ds(ch * CHUNK, CHUNK)].reshape(CROWS, 128)
            lat_turned[ch] = jnp.transpose(lat_c)[0:64]

            def block(b, accs):
                mix_acc, u_acc = accs
                keys_grads = wide(16, 144, b)
                scores = dot(queries(ch), keys_grads)
                d = jnp.exp(scores - dnorm[b, 0:1, :])
                e = jnp.exp(scores - enorm[pl.ds(ch * CHUNK, CHUNK)].reshape(CROWS, 128)[:, 0:1])
                dec[ch, b] = d
                enc[ch, b] = e
                mix_acc = mix_acc + dot_lanes(d.astype(BF16), keys_grads)
                u_acc = u_acc + dot_lanes(e.astype(BF16), wide(144, 272, b))
                return mix_acc, u_acc

            blank = jnp.zeros((CROWS, 128), F32)
            mix_acc, u_acc = lax.fori_loop(0, NB, block, (blank, blank))
            mixu[pl.ds(ch * CHUNK, CHUNK)] = jnp.where(left, u_acc, mix_acc).reshape(CHUNK, BLOCK, 128)
            scatter(order, mixu, from_core, summed, from_z, s_core, r_core, s_z, r_z, mixu_send)

        query_acc[...] = jnp.zeros((4, CROWS, 128), F32)

        def decoder_block(b):
            def totals(ch, total):
                dg = dot(outs(ch), wide(16, 144, b))
                dgrad[ch] = dg
                return total + jnp.sum(dec[ch, b] * dg, axis=0, keepdims=True)

            row_total = lax.fori_loop(0, 4, totals, jnp.zeros((1, NW), F32))

            def grads(ch, acc):
                ds = (dec[ch, b] * (dgrad[ch] - row_total)).astype(BF16)
                query_acc[ch] = query_acc[ch] + dot_lanes(ds, wide(16, 144, b))
                return acc + dot(lat_turned[ch], ds)

            keys_t[b] = lax.fori_loop(0, 4, grads, jnp.zeros((64, NW), F32))
            values_t[b] = jnp.zeros((64, NW), F32)


        own_mix = scatter_wait(from_z, summed, s_z, r_z)
        own_u = scatter_wait(from_z_u, summed_u, s_zu, r_zu)
        lane = iota((BLOCK, 128), 1)
        mix_half = jnp.concatenate([pltpu.roll(own_mix, HEAD_DIM, 1), own_mix], axis=0).astype(BF16).astype(F32)
        own = jnp.concatenate([own_u, pltpu.roll(own_u, HEAD_DIM, 1)], axis=0)
        column_total = jnp.sum(jnp.where(lane < HEAD_DIM, own * mix_half, 0.0), axis=1, keepdims=True)
        one, two, three = three_terms(column_total)
        mix_all[member] = jnp.where(
            lane < HEAD_DIM, mix_half,
            jnp.where(lane == 64, one, jnp.where(lane == 65, two, jnp.where(lane == 66, three, 0.0))),
        ).astype(BF16)
        gather_send(mix_all, s_mix, r_mix)

        loop(0, NB, decoder_block)

        gather_relay(mix_all, s_mix, r_mix)

        for order in range(4):
            cc, zc, ch = chunk_of(order)
            if order in (1, 2):
                gather_sibling(mix_all, s_mix, r_mix, zc)
            mix_turned = jnp.transpose(mix_all[pl.ds(ch * CHUNK, CHUNK)].reshape(CROWS, 128))[0:64]

            def block2(b, acc):
                eg = dot(mix_all[pl.ds(ch * CHUNK, CHUNK)].reshape(CROWS, 128), wide(144, 272, b))
                e = enc[ch, b]
                ds = (e * eg).astype(BF16)
                values_t[b] = values_t[b] + dot(mix_turned, e.astype(BF16))
                keys_t[b] = keys_t[b] + dot(lat_turned[ch], ds)
                return acc + dot_lanes(ds, wide(16, 144, b))

            acc = lax.fori_loop(0, NB, block2, query_acc[ch]) * 0.125
            acc = acc.reshape(CHUNK, BLOCK, 128)
            upper = acc[:, 0:32, :].reshape(CHUNK * 32, 128)
            lower = pltpu.roll(acc[:, 32:64, :].reshape(CHUNK * 32, 128), HEAD_DIM, 1)
            packed = jnp.where(iota((CHUNK * 32, 128), 1) < HEAD_DIM, upper, lower)
            lg_part[pl.ds(ch * CHUNK, CHUNK)] = packed.reshape(CHUNK, 32, 128)
            scatter(order, lg_part, lg_core, lg_summed, lg_z, s_core2, r_core2, s_z2, r_z2)

        for t in range(SLOTS):
            b, at = t // 16, 128 * (t % 16)
            kv_send[t, 0:64, :] = keys_t[b, :, at : at + 128].astype(BF16)
            kv_send[t, 64:128, :] = values_t[b, :, at : at + 128].astype(BF16)

    def kv_copy(t, h):
        return remote(kv_send.at[t], kv_got.at[h], s_kv.at[t], r_kv.at[h], in_plane(t))

    def lg_copy(t, h):
        row = ((t // 4) % 2) * 16 + ((t % 4) // 2) * 8
        return remote(lg_own.at[pl.ds(row, 8)], lg_got.at[h], s_lg.at[t], r_lg.at[h], in_plane(t))

    @pl.when(head < HEADS)
    def _():
        loop(1, SLOTS, lambda k: kv_copy((place + k) % SLOTS, head).start())
        kv_got[head] = kv_send[place]

        def z_copy2(z_to, z_from):
            return remote(
                lg_summed.at[z_to], lg_z.at[z_from], s_z2.at[z_to], r_z2.at[z_from], in_column(c * 8 + z_to)
            )

        loop(1, 8, lambda k: z_copy2(z, (z + k) % 8).wait_recv())
        result = lg_z[0]
        for i in range(1, 8):
            result = result + lg_z[i]
        lg_own[...] = result
        for k in PLANE_ORDER:
            lg_copy(plane_at(k), head).start()
        row = pl.multiple_of((x % 2) * 16 + (y // 2) * 8, 8)
        lg_got[head] = lg_own[pl.ds(row, 8), :]

    def from_heads(copy):
        def body(k):
            src = (place + k) % SLOTS

            @pl.when(head_at(src) < HEADS)
            def _():
                copy(place, head_at(src)).wait_recv()

        loop(1, SLOTS, body)

    from_heads(kv_copy)
    kv_out[...] = kv_got[...]
    from_heads(lg_copy)
    lg_out[...] = lg_got[...]

    def sent(k):
        to = (place + k) % SLOTS

        @pl.when(head_at(to) < HEADS)
        def _():
            lat_copy(to, place).wait_send()
            pts_copy(to, place).wait_send()

    loop(1, SLOTS, sent)

    @pl.when(head < HEADS)
    def _():
        def sent_column(k):
            t = (place + k) % SLOTS
            kv_copy(t, head).wait_send()
            lg_copy(t, head).wait_send()

        loop(1, SLOTS, sent_column)
        to_sibling(lat, s_all, r_all, z).wait_send()
        to_sibling(mix_all, s_mix, r_mix, z).wait_send()

        def sent_z(k):
            zz = (z + k) % 8
            for buf, s, r in ((lat, s_all, r_all), (mix_all, s_mix, r_mix)):
                along_z(buf, s, r, zz).wait_send()
                to_sibling(buf, s, r, zz).wait_send()
            remote(summed.at[zz], from_z.at[z], s_z.at[zz], r_z.at[z], in_column(c * 8 + zz)).wait_send()
            remote(summed_u.at[zz], from_z_u.at[z], s_zu.at[zz], r_zu.at[z], in_column(c * 8 + zz)).wait_send()
            remote(lg_summed.at[zz], lg_z.at[z], s_z2.at[zz], r_z2.at[z], in_column(c * 8 + zz)).wait_send()

        loop(1, 8, sent_z)
        sibling = in_column((1 - c) * 8 + z)
        for order in range(2):
            zc = (1 - z // 4) if order == 0 else z // 4
            g = (1 - c) * 8 + zc * 4
            remote(
                mixu.at[pl.ds(g, CHUNK)], from_core.at[pl.ds(zc * 4, CHUNK)], s_core.at[order], r_core.at[zc], sibling
            ).wait_send()
            remote(
                lg_part.at[pl.ds(g, CHUNK)], lg_core.at[pl.ds(zc * 4, CHUNK)], s_core2.at[order], r_core2.at[zc], sibling
            ).wait_send()


def unpack(kv_ref, lg_ref, kout_ref, vout_ref, lgout_ref):
    pa, pb = lax.axis_index("pa"), lax.axis_index("pb")
    high, y = pa // 8 == 1, pb // 4
    for p in range(HEADS // 2):
        for i, ref in enumerate((kout_ref, vout_ref)):
            both = jnp.concatenate(
                [kv_ref[2 * p, 64 * i : 64 * i + 64, :], kv_ref[2 * p + 1, 64 * i : 64 * i + 64, :]], axis=0
            )
            ref[:, 128 * p : 128 * p + 128] = jnp.transpose(both)
    left8 = iota((8, 128), 1) < HEAD_DIM
    for p in range(HEADS // 2):
        a, b = lg_ref[2 * p], lg_ref[2 * p + 1]
        a = jnp.where(high, pltpu.roll(a, HEAD_DIM, 1), a)
        b = jnp.where(high, b, pltpu.roll(b, HEAD_DIM, 1))
        both = jnp.where(left8, a, b)
        lgout_ref[:, 128 * p : 128 * p + 128] = jnp.where(y % 2 == 0, both[0:4], both[4:8])


def shards(point_keys, point_values, out_grad, decoder_norm, latent_query, latent_out, encoder_norm):
    vmem = pl.BlockSpec(memory_space=pltpu.VMEM)
    sem = pltpu.SemaphoreType.DMA
    scratch = [
        pltpu.VMEM((PTS, 768), BF16), pltpu.VMEM((PTS, 768), BF16), pltpu.VMEM((PTS, 768), BF16),
        pltpu.VMEM((HEADS, PTS), F32), pltpu.VMEM((4, 768), BF16), pltpu.VMEM((4, 768), BF16),
        pltpu.VMEM((HEADS, 1024), F32), sem((7,)),
        pltpu.VMEM((HEADS, 16, 128), BF16),
        pltpu.VMEM((HEADS, 208, 128), BF16),
        pltpu.VMEM((2, 16, 768), F32),
        pltpu.VMEM((SLOTS, 16, 128), BF16),
        pltpu.VMEM((SLOTS, 272, 128), BF16),
        pltpu.VMEM((NB, 8, NW), F32),
        pltpu.VMEM((SLOTS, BLOCK, 128), F32),
        pltpu.VMEM((SLOTS, BLOCK, 128), BF16),
        pltpu.VMEM((4, 64, CROWS), BF16),
        pltpu.VMEM((4, NB, CROWS, NW), F32),
        pltpu.VMEM((4, NB, CROWS, NW), F32),
        pltpu.VMEM((4, CROWS, NW), F32),
        pltpu.VMEM((4, CROWS, 128), F32),
        pltpu.VMEM((SLOTS, BLOCK, 128), F32),
        pltpu.VMEM((8, BLOCK, 128), F32),
        pltpu.VMEM((8, 32, 128), F32),
        pltpu.VMEM((8, 32, 128), F32),
        pltpu.VMEM((8, 32, 128), BF16),
        pltpu.VMEM((8, 32, 128), BF16),
        pltpu.VMEM((SLOTS, BLOCK, 128), BF16),
        pltpu.VMEM((NB, 64, NW), F32),
        pltpu.VMEM((NB, 64, NW), F32),
        pltpu.VMEM((SLOTS, 32, 128), F32),
        pltpu.VMEM((8, 32, 128), F32),
        pltpu.VMEM((8, 32, 128), F32),
        pltpu.VMEM((8, 32, 128), F32),
        pltpu.VMEM((32, 128), F32),
        pltpu.VMEM((SLOTS, 128, 128), BF16),
        pltpu.VMEM((HEADS, 128, 128), BF16),
        pltpu.VMEM((HEADS, 8, 128), F32),
        sem((SLOTS,)), sem((SLOTS,)), sem((SLOTS,)), sem((SLOTS,)),
        sem((SLOTS,)), sem((SLOTS,)), sem((2,)), sem((2,)), sem((8,)), sem((8,)), sem((8,)), sem((8,)),
        sem((SLOTS,)), sem((SLOTS,)), sem((2,)), sem((2,)), sem((8,)), sem((8,)),
        sem((SLOTS,)), sem((SLOTS,)), sem((SLOTS,)), sem((SLOTS,)),
    ]
    kv, lg = pl.pallas_call(
        kernel,
        out_shape=(
            pltpu.VMEM((HEADS, 128, 128), BF16),
            pltpu.VMEM((HEADS, 8, 128), F32),
        ),
        in_specs=[pl.BlockSpec(memory_space=pl.ANY)] * 7,
        out_specs=(vmem, vmem),
        scratch_shapes=scratch,
        compiler_params=pltpu.CompilerParams(
            collective_id=0, has_side_effects=True, vmem_limit_bytes=56 * 1024 * 1024
        ),
        name="routing_backward",
    )(point_keys, point_values, out_grad, decoder_norm, latent_query, latent_out, encoder_norm)
    return pl.pallas_call(
        unpack,
        out_shape=(
            jax.ShapeDtypeStruct(point_keys.shape, BF16),
            jax.ShapeDtypeStruct(point_values.shape, BF16),
            jax.ShapeDtypeStruct(latent_query.shape, F32),
        ),
        in_specs=[vmem] * 2,
        out_specs=(vmem, vmem, vmem),
        compiler_params=pltpu.CompilerParams(vmem_limit_bytes=8 * 1024 * 1024),
        name="unpack",
    )(kv, lg)


def solution(mesh):
    both = ("pa", "pb")
    rows = P(both, None)
    return jax.shard_map(
        shards,
        mesh=mesh,
        in_specs=(rows, rows, rows, P(None, both), rows, rows, P()),
        out_specs=(rows, rows, rows),
        check_vma=False,
    )
```
